32 devices in a mesh: runs: 2 (over x), gy: 16 (over z, y, core).
Axes of the slice: x: 2, y: 2, z: 4, core: 2. Of those that a mesh axis runs over, the one named last changes fastest.
Arguments:
- depth: float32 [1024, 1920], P(('runs', 'gy')), parts along dimension 0, may hold values from 0.02 to 3
- flux_east: float32 [1024, 1920], P(('runs', 'gy')), parts along dimension 0, may hold values from -2 to 2
- flux_south: float32 [1024, 1920], P(('runs', 'gy')), parts along dimension 0, may hold values from -2 to 2
- river_section: float32 [4096], P(('runs', 'gy')), parts along dimension 0, may hold values from 0 to 2
- bed_level: float32 [512, 1920], P('gy'), may hold values from -3 to 3
- rough_class: int32 [512, 1920], P('gy'), may hold values from 0 to 7
- manning_table: float32 [8], replicated, may hold values from 0.02 to 0.15
- bank_cell: int32 [4, 2048], P(None, 'gy'), may hold values from 0 to 983039, as said below
Outputs:
- depth_out: float32 [1024, 1920], P(('runs', 'gy')), parts along dimension 0
- east_out: float32 [1024, 1920], P(('runs', 'gy')), parts along dimension 0
- south_out: float32 [1024, 1920], P(('runs', 'gy')), parts along dimension 0
- section_out: float32 [4096], P(('runs', 'gy')), parts along dimension 0
The draws below stay inside these ranges and needn't reach their ends.
There are 2 independent parts, one for each index of `runs`. The reference program is written for one: setup_inputs(seed, part) draws one part's arguments, and reference() takes and returns one part's arrays. A program takes and returns all parts, laid end to end along the dimension named above; an argument that names none is the same for every part. Nothing has to cross between parts.
Inputs may be any that keep to these rules, and one draw needn't show every extreme that they name: `bank_cell`: the 4 corridor cells of a node are consecutive flat indices row * 1920 + column within one map row. Node n is owned by gy index o = n // 128, and all its corridor cells lie in map rows from max((o - 1) * 32, 0) to min((o + 2) * 32, 512) - 1.
All inputs are finite; a program needn't handle non-finite values.
Results may differ from the reference program's by a relative error of at most 0.00013.
Values sent between devices are 32-bit elements; how exact they have to be, the bound alone decides.
A program may use at most 64 MiB of HBM per device.

```python
import math
import jax
import jax.numpy as jnp

RY = 32
NX = 1920
NODE_DEV = 128
K = 4
CLASSES = 8
STEPS = 4
NY = 512
NODES = 2048


def draw_bank_cell(key, part):
    tiles = NODES // NODE_DEV
    key_start, key_walk, key_jitter = jax.random.split(key, 3)
    node = jnp.arange(NODES, dtype=jnp.int32)
    owner = node // NODE_DEV
    place = node % NODE_DEV
    jitter = jax.random.randint(key_jitter, (NODES,), 0, 2).astype(jnp.int32)
    row = (owner - 1) * RY + place * 3 * RY // NODE_DEV + jitter
    row = jnp.clip(row, jnp.maximum((owner - 1) * RY, 0), jnp.minimum((owner + 2) * RY - 1, NY - 1))
    start = jax.random.randint(key_start, (tiles, 1), 0, NX - K + 1).astype(jnp.int32)
    moves = jax.random.randint(key_walk, (tiles, NODE_DEV), -2, 3).astype(jnp.int32)
    column = jnp.clip(start + jnp.cumsum(moves, axis=1), 0, NX - K).reshape(-1).astype(jnp.int32)
    row = row.at[0].set(0).at[NODES - 1].set(NY - 1)
    column = column.at[0].set(0).at[NODES - 1].set(NX - K)
    flat = row * NX + column
    return (flat[None, :] + jnp.arange(K, dtype=jnp.int32)[:, None]).astype(jnp.int32)


def plant(result, rng, low, top_value):
    dims = result.shape
    index_at = [jax.random.randint(jax.random.fold_in(rng, axis), (), 0, dims[axis]) for axis in range(len(dims))]
    result = result.at[tuple(index_at)].set(low)
    longest = dims.index(max(dims))
    index_at[longest] = (index_at[longest] + 1) % dims[longest]
    return result.at[tuple(index_at)].set(top_value)


def shard_levels(stream_key, dims, cuts, low, largest):
    def one(position, blocks):
        heights = jax.random.uniform(jax.random.fold_in(jax.random.fold_in(stream_key, 6), position), (blocks,), jnp.float32, low / len(cuts), largest / len(cuts))
        return jnp.repeat(jnp.exp(heights), dims[position] // blocks).reshape((-1,) + (1,) * (len(dims) - position - 1))

    factor_of = one(*cuts[0])
    for cut in cuts[1:]:
        factor_of = factor_of * one(*cut)
    return factor_of


def noise(rng, shape, scale, reach, cuts=(), held_as=jnp.bfloat16):
    level = shard_levels(rng, shape, cuts, -0.22, 0.18) if cuts else 1.0
    result = jax.random.normal(rng, shape, jnp.float32) * scale * level
    return jnp.minimum(jnp.maximum(result, -reach), reach).astype(held_as)


def setup_inputs(seed: int = 0, part: int = 0) -> dict:
    key_of = jax.random.split(jax.random.key(seed), 9)
    part_splits = jax.random.split(jax.random.fold_in(key_of[8], part), 9)
    return {
        "depth": jnp.clip(jnp.exp(math.log(3.0) - 5.0106353 * jax.random.uniform(part_splits[0], (NY, NX), jnp.float32) ** shard_levels(part_splits[0], (NY, NX), ((0, 16),), -0.2, 0.2)), 0.02, 3.0),
        "flux_east": noise(part_splits[1], (NY, NX), 0.3, 2.0, ((0, 16),), jnp.float32),
        "flux_south": noise(part_splits[2], (NY, NX), 0.3, 2.0, ((0, 16),), jnp.float32),
        "river_section": jnp.clip(2.0 * jax.random.uniform(part_splits[3], (NODES,), jnp.float32) ** shard_levels(part_splits[3], (NODES,), ((0, 16),), -0.2, 0.2), 0.0, 2.0),
        "bed_level": noise(key_of[4], (NY, NX), 0.5, 3.0, ((0, 16),), jnp.float32),
        "rough_class": plant(jax.random.randint(key_of[5], (NY, NX), 0, CLASSES), jax.random.fold_in(key_of[5], 1), 0, CLASSES - 1).astype(jnp.int32),
        "manning_table": jnp.clip(jnp.exp(jax.random.uniform(key_of[6], (CLASSES,), jnp.float32, math.log(0.02), math.log(0.15))), 0.02, 0.15),
        "bank_cell": draw_bank_cell(jax.random.fold_in(key_of[8], 71), part),
    }


GRAV = 9.81
TSTEP = 8.0
CELL = 90.0
FLOOR = 0.05
BANK_COEF = 200.0
CELL_AREA = 8100.0
NODE_AREA = 20000.0


def face_flux(flux, surf_a, surf_b, bed_a, bed_b, mann_a, mann_b):
    flow_depth = jnp.maximum(jnp.maximum(surf_a, surf_b) - jnp.maximum(bed_a, bed_b), FLOOR)
    mean_mann = 0.5 * (mann_a + mann_b)
    driven = flux - GRAV * flow_depth * TSTEP * (surf_b - surf_a) / CELL
    damping = 1.0 + GRAV * TSTEP * mean_mann * mean_mann * jnp.abs(flux) / jnp.power(flow_depth, 7.0 / 3.0)
    return driven / damping


def reference(depth, flux_east, flux_south, river_section, bed_level, rough_class, manning_table, bank_cell):
    manning = manning_table[rough_class]
    rows_all, cols_all = depth.shape
    for substep in range(STEPS):
        surface = depth + bed_level
        east_part = face_flux(flux_east[:, :-1], surface[:, :-1], surface[:, 1:], bed_level[:, :-1], bed_level[:, 1:], manning[:, :-1], manning[:, 1:])
        flux_east = jnp.concatenate([east_part, jnp.zeros((rows_all, 1), jnp.float32)], axis=1)
        south_part = face_flux(flux_south[:-1], surface[:-1], surface[1:], bed_level[:-1], bed_level[1:], manning[:-1], manning[1:])
        flux_south = jnp.concatenate([south_part, jnp.zeros((1, cols_all), jnp.float32)], axis=0)
        surf_flat = surface.reshape(-1)
        bank_flow = BANK_COEF * (river_section[None, :] - surf_flat[bank_cell])
        source = jnp.zeros((rows_all * cols_all,), jnp.float32).at[bank_cell.reshape(-1)].add(bank_flow.reshape(-1)).reshape(rows_all, cols_all)
        east_in = jnp.concatenate([jnp.zeros((rows_all, 1), jnp.float32), flux_east[:, :-1]], axis=1)
        south_in = jnp.concatenate([jnp.zeros((1, cols_all), jnp.float32), flux_south[:-1]], axis=0)
        depth = depth + TSTEP / CELL * (east_in - flux_east + south_in - flux_south) + TSTEP * source / CELL_AREA
        river_section = river_section - TSTEP * jnp.sum(bank_flow, axis=0) / NODE_AREA
    return depth, flux_east, flux_south, river_section
```

```python
import jax
import jax.numpy as jnp
from jax import lax
from jax.experimental import pallas as pl
from jax.experimental.pallas import tpu as pltpu
from jax.sharding import PartitionSpec as P

STEPS = 4
HALO = STEPS
LANES = 128

GRAV = 9.81
TSTEP = 8.0
CELL = 90.0
FLOOR = 0.05
BANK_COEF = 200.0
CELL_AREA = 8100.0
NODE_AREA = 20000.0

MESH = pl.DeviceIdType.MESH
VMEM_BYTES = 40 * 1024 * 1024
FAR = -float(1 << 24)


def send(src, dst, send_sem, recv_sem, target):
    return pltpu.make_async_remote_copy(
        src_ref=src,
        dst_ref=dst,
        send_sem=send_sem,
        recv_sem=recv_sem,
        device_id={"gy": target},
        device_id_type=MESH,
    )


def exchange_kernel(*refs):
    firsts, lasts = refs[0:5], refs[5:10]
    section, cells = refs[10:12]
    below_out, above_out, nodes_out = refs[12:15]
    up, down, below, above, mine, nodes, ssem, rsem, nssem, nrsem = refs[15:]
    me = lax.axis_index("gy")
    count = lax.axis_size("gy")
    offsets = (-2, -1, 1, 2)

    def there(offset):
        return (me + offset >= 0) & (me + offset < count)

    barrier = pltpu.get_barrier_semaphore()
    for offset in offsets:
        @pl.when(there(offset))
        def _():
            pl.semaphore_signal(
                barrier, inc=1, device_id={"gy": me + offset}, device_id_type=MESH
            )

    for i in range(5):
        up[i] = firsts[i][:HALO, :].astype(jnp.float32)
        down[i] = lasts[i][8 - HALO :, :].astype(jnp.float32)
    mine[0:1, :] = section[...]
    mine[1:2, :] = cells[0:1, :].astype(jnp.float32)

    pl.semaphore_wait(barrier, jnp.minimum(me, 2) + jnp.minimum(count - 1 - me, 2))

    to_prev = send(up, below, ssem.at[0], rsem.at[0], me - 1)
    to_next = send(down, above, ssem.at[1], rsem.at[1], me + 1)
    to_nodes = [
        send(mine, nodes.at[i], nssem.at[i], nrsem.at[i], me - offset)
        for i, offset in enumerate(offsets)
    ]

    for i, offset in enumerate(offsets):
        @pl.when(there(-offset))
        def _():
            to_nodes[i].start()

    @pl.when(there(-1))
    def _():
        to_prev.start()

    @pl.when(there(1))
    def _():
        to_next.start()

    nodes_out[2] = mine[...]
    for i, offset in enumerate(offsets):
        slot = offset + 2

        @pl.when(there(offset))
        def _():
            to_nodes[i].wait_recv()
            nodes_out[slot] = nodes[i]

        @pl.when(jnp.logical_not(there(offset)))
        def _():
            nodes_out[slot, 0:1, :] = jnp.zeros((1, nodes_out.shape[2]), jnp.float32)
            nodes_out[slot, 1:2, :] = jnp.full((1, nodes_out.shape[2]), FAR, jnp.float32)

    @pl.when(there(1))
    def _():
        to_prev.wait_recv()
        below_out[...] = below[...]

    @pl.when(jnp.logical_not(there(1)))
    def _():
        below_out[...] = jnp.zeros_like(below_out)

    @pl.when(there(-1))
    def _():
        to_next.wait_recv()
        above_out[...] = above[...]

    @pl.when(jnp.logical_not(there(-1)))
    def _():
        above_out[...] = jnp.zeros_like(above_out)

    @pl.when(there(-1))
    def _():
        to_prev.wait_send()

    @pl.when(there(1))
    def _():
        to_next.wait_send()

    for i, offset in enumerate(offsets):
        @pl.when(there(-offset))
        def _():
            to_nodes[i].wait_send()


def exchange(arrays, section, bank_cell):
    rows, columns = arrays[0].shape
    owned = section.shape[1]
    strip = (5, HALO, columns)
    first = pl.BlockSpec((8, columns), lambda i: (0, 0))
    last = pl.BlockSpec((8, columns), lambda i: (rows // 8 - 1, 0))
    whole = lambda *shape: pl.BlockSpec(shape, lambda i: (0,) * len(shape))
    return pl.pallas_call(
        exchange_kernel,
        grid=(1,),
        out_shape=[
            jax.ShapeDtypeStruct(strip, jnp.float32),
            jax.ShapeDtypeStruct(strip, jnp.float32),
            jax.ShapeDtypeStruct((5, 2, owned), jnp.float32),
        ],
        in_specs=[first] * 5
        + [last] * 5
        + [whole(1, owned), whole(*bank_cell.shape)],
        out_specs=[whole(*strip), whole(*strip), whole(5, 2, owned)],
        scratch_shapes=[pltpu.VMEM(strip, jnp.float32)] * 4
        + [
            pltpu.VMEM((2, owned), jnp.float32),
            pltpu.VMEM((4, 2, owned), jnp.float32),
            pltpu.SemaphoreType.DMA((2,)),
            pltpu.SemaphoreType.DMA((2,)),
            pltpu.SemaphoreType.DMA((4,)),
            pltpu.SemaphoreType.DMA((4,)),
        ],
        compiler_params=pltpu.CompilerParams(collective_id=0, has_side_effects=True),
        name="exchange",
    )(*arrays, *arrays, section, bank_cell)


def thirds(value):
    high = value.astype(jnp.bfloat16).astype(jnp.float32)
    rest = value - high
    mid = rest.astype(jnp.bfloat16).astype(jnp.float32)
    return high, mid, rest - mid


def steps_kernel(
    table,
    pos,
    depth,
    flux_east,
    flux_south,
    bed_in,
    rough_in,
    below,
    above,
    nodes,
    depth_out,
    east_out,
    south_out,
    part_out,
    surf,
    fe,
    fs,
    bed,
    mann,
    max_e,
    max_s,
    drag_e,
    drag_s,
    tally,
    number,
    number4,
    gained,
    partial,
):
    me = pos[0]
    tiles = pos[1]
    rows, columns = depth.shape
    ext = rows + 2 * HALO
    chunks = columns // LANES
    owned = nodes.shape[2]
    keep = 1.0 - TSTEP * BANK_COEF * 4.0 / NODE_AREA
    gain = TSTEP * BANK_COEF / NODE_AREA
    into = TSTEP * BANK_COEF / CELL_AREA

    def at(chunk, shift=0):
        start = LANES * (chunk + 1) + shift
        return slice(start, start + LANES)

    def south(value):
        return pltpu.roll(value, ext - 1, 0)

    def north(value):
        return pltpu.roll(value, 1, 0)

    for ref in (surf, fe, bed, mann, tally, number):
        ref[:, :LANES] = jnp.zeros((ext, LANES), jnp.float32)
        ref[:, LANES * (chunks + 1) :] = jnp.zeros((ext, LANES), jnp.float32)

    def extended(source, index, chunk):
        lanes = slice(LANES * chunk, LANES * (chunk + 1))
        return jnp.concatenate(
            [source[:, lanes].astype(jnp.float32), below[index, :, lanes], above[index, :, lanes]],
            axis=0,
        )

    row_id = lax.broadcasted_iota(jnp.int32, (ext, LANES), 0)
    lane_id = lax.broadcasted_iota(jnp.int32, (ext, LANES), 1)
    south_open = jnp.logical_not(
        ((row_id == ext - 1) & (me == 0)) | ((row_id == rows - 1) & (me == tiles - 1))
    )

    for c in range(chunks):
        bed_c = extended(bed_in, 3, c)
        bed[:, at(c)] = bed_c
        surf[:, at(c)] = extended(depth, 0, c) + bed_c
        fe[:, at(c)] = extended(flux_east, 1, c)
        fs[:, at(c)] = extended(flux_south, 2, c)
        rough = extended(rough_in, 4, c)
        value = jnp.zeros((ext, LANES), jnp.float32)
        for klass in range(table.shape[0]):
            value = jnp.where(rough == float(klass), table[klass], value)
        mann[:, at(c)] = value
    for c in range(chunks):
        bed_c, mann_c = bed[:, at(c)], mann[:, at(c)]
        max_e[:, at(c)] = jnp.maximum(bed_c, bed[:, at(c, 1)])
        max_s[:, at(c)] = jnp.maximum(bed_c, south(bed_c))
        mean_e = 0.5 * (mann_c + mann[:, at(c, 1)])
        mean_s = 0.5 * (mann_c + south(mann_c))
        drag_e[:, at(c)] = GRAV * TSTEP * mean_e * mean_e
        drag_s[:, at(c)] = GRAV * TSTEP * mean_s * mean_s
        gained[:, at(c)] = jnp.zeros((ext, LANES), jnp.float32)

    section = jnp.concatenate([nodes[i, 0:1, :] for i in range(5)], axis=1)
    cell = jnp.concatenate([nodes[i, 1:2, :] for i in range(5)], axis=1).astype(jnp.int32)
    local = cell - (me * rows - HALO) * columns
    valid = (local >= 0) & (local < ext * columns)
    local = jnp.where(valid, local, 0)
    from_top = ((local.astype(jnp.float32) + 0.5) * (1.0 / columns)).astype(jnp.int32)
    column = local - from_top * columns
    row = jnp.where(from_top < HALO, from_top + ext - HALO, from_top - HALO)
    place = jnp.where(valid, (column >> 7) * ext + row, -1)
    lane = column & (LANES - 1)
    total = 5 * owned
    blocks = chunks * ext
    blocks_pad = -(-blocks // LANES) * LANES
    hit = (lax.broadcasted_iota(jnp.int32, (blocks_pad, total), 0) == place)
    hit = jnp.where(hit, 1.0, 0.0).astype(jnp.bfloat16)
    lane_hit = lax.broadcasted_iota(jnp.int32, (LANES, total), 0) == lane
    parts = [jnp.where(lane_hit, part, 0.0) for part in thirds(section)]
    parts.append(jnp.where(lane_hit, 1.0, 0.0))
    weights = jnp.concatenate(parts, axis=0).astype(jnp.bfloat16)
    spread = lax.dot_general(
        hit, weights, (((1,), (1,)), ((), ())), preferred_element_type=jnp.float32
    )
    for c in range(chunks):
        block = spread[c * ext : (c + 1) * ext]
        tally[:, at(c)] = (
            block[:, :LANES] + block[:, LANES : 2 * LANES] + block[:, 2 * LANES : 3 * LANES]
        )
        number[:, at(c)] = block[:, 3 * LANES :]
    for c in range(chunks):
        number4[:, at(c)] = (
            number[:, at(c)] + number[:, at(c, -1)] + number[:, at(c, -2)] + number[:, at(c, -3)]
        )

    def face(flux, surf_a, surf_b, bed_top, drag):
        flow_depth = jnp.maximum(jnp.maximum(surf_a, surf_b) - bed_top, FLOOR)
        driven = flux - (GRAV * TSTEP / CELL) * flow_depth * (surf_b - surf_a)
        damping = 1.0 + drag * jnp.abs(flux) * jnp.exp(jnp.log(flow_depth) * (-7.0 / 3.0))
        return driven / damping

    def substep(_, carry):
        for c in reversed(range(chunks)):
            here = surf[:, at(c)]
            east = surf[:, at(c, 1)]
            new_east = face(fe[:, at(c)], here, east, max_e[:, at(c)], drag_e[:, at(c)])
            if c == chunks - 1:
                new_east = jnp.where(lane_id == LANES - 1, 0.0, new_east)
            fe[:, at(c)] = new_east
            new_south = face(
                fs[:, at(c)], here, south(here), max_s[:, at(c)], drag_s[:, at(c)]
            )
            new_south = jnp.where(south_open, new_south, 0.0)
            fs[:, at(c)] = new_south
            own = tally[:, at(c)]
            tally4 = own + tally[:, at(c, -1)] + tally[:, at(c, -2)] + tally[:, at(c, -3)]
            box = gain * (here + east + surf[:, at(c, 2)] + surf[:, at(c, 3)])
            tally[:, at(c)] = keep * own + number[:, at(c)] * box
            gained[:, at(c)] = keep * gained[:, at(c)] + box
            partial[:, at(c)] = (
                here
                + into * (tally4 - number4[:, at(c)] * here)
                + (TSTEP / CELL) * (north(new_south) - new_south - new_east)
            )
        for c in range(chunks):
            surf[:, at(c)] = partial[:, at(c)] + (TSTEP / CELL) * fe[:, at(c, -1)]
        return carry

    lax.fori_loop(0, STEPS, substep, 0)

    for c in range(chunks):
        lanes = slice(LANES * c, LANES * (c + 1))
        depth_out[:, lanes] = surf[:rows, at(c)] - bed[:rows, at(c)]
        east_out[:, lanes] = fe[:rows, at(c)]
        south_out[:, lanes] = fs[:rows, at(c)]

    flat = jnp.concatenate(
        [jnp.where(row_id < rows, gained[:, at(c)], 0.0) for c in range(chunks)]
        + ([jnp.zeros((blocks_pad - blocks, LANES), jnp.float32)] if blocks_pad > blocks else []),
        axis=0,
    )
    near = slice(owned, 4 * owned)
    turned = jnp.concatenate(thirds(flat.T), axis=0).astype(jnp.bfloat16)
    picked = jnp.dot(turned, hit[:, near], preferred_element_type=jnp.float32)
    picked = picked[:LANES] + picked[LANES : 2 * LANES] + picked[2 * LANES :]
    picked = jnp.sum(jnp.where(lane_hit[:, near], picked, 0.0), axis=0, keepdims=True)
    inside = (valid & (row < rows))[:, near]
    final = jnp.where(inside, keep**STEPS * section[:, near] + picked, 0.0)
    for i in range(3):
        part_out[i] = final[:, i * owned : (i + 1) * owned]


def run_steps(table, pos, depth, flux_east, flux_south, bed, rough, below, above, nodes):
    rows, columns = depth.shape
    owned = nodes.shape[2]
    ext = rows + 2 * HALO
    vmem = pl.BlockSpec(memory_space=pltpu.VMEM)
    smem = pl.BlockSpec(memory_space=pltpu.SMEM)
    tile = jax.ShapeDtypeStruct((rows, columns), jnp.float32)
    return pl.pallas_call(
        steps_kernel,
        out_shape=[tile, tile, tile, jax.ShapeDtypeStruct((3, 1, owned), jnp.float32)],
        in_specs=[smem, smem] + [vmem] * 8,
        out_specs=[vmem] * 4,
        scratch_shapes=[pltpu.VMEM((ext, columns + 2 * LANES), jnp.float32)] * 14,
        compiler_params=pltpu.CompilerParams(vmem_limit_bytes=VMEM_BYTES),
        name="substeps",
    )(table, pos, depth, flux_east, flux_south, bed, rough, below, above, nodes)


def return_kernel(part, out, low, high, ssem, rsem):
    me = lax.axis_index("gy")
    count = lax.axis_size("gy")
    has_prev = me > 0
    has_next = me < count - 1
    barrier = pltpu.get_barrier_semaphore()

    @pl.when(has_prev)
    def _():
        pl.semaphore_signal(barrier, inc=1, device_id={"gy": me - 1}, device_id_type=MESH)

    @pl.when(has_next)
    def _():
        pl.semaphore_signal(barrier, inc=1, device_id={"gy": me + 1}, device_id_type=MESH)

    pl.semaphore_wait(barrier, jnp.minimum(me, 1) + jnp.minimum(count - 1 - me, 1))

    to_prev = send(part.at[0], high, ssem.at[0], rsem.at[0], me - 1)
    to_next = send(part.at[2], low, ssem.at[1], rsem.at[1], me + 1)

    @pl.when(has_prev)
    def _():
        to_prev.start()

    @pl.when(has_next)
    def _():
        to_next.start()

    out[...] = part[1]

    @pl.when(has_next)
    def _():
        to_prev.wait_recv()
        out[...] += high[...]

    @pl.when(has_prev)
    def _():
        to_next.wait_recv()
        out[...] += low[...]

    @pl.when(has_prev)
    def _():
        to_prev.wait_send()

    @pl.when(has_next)
    def _():
        to_next.wait_send()


def return_parts(part):
    shape = part.shape[1:]
    vmem = pl.BlockSpec(memory_space=pltpu.VMEM)
    return pl.pallas_call(
        return_kernel,
        out_shape=jax.ShapeDtypeStruct(shape, jnp.float32),
        in_specs=[vmem],
        out_specs=vmem,
        scratch_shapes=[pltpu.VMEM(shape, jnp.float32)] * 2
        + [pltpu.SemaphoreType.DMA((2,)), pltpu.SemaphoreType.DMA((2,))],
        compiler_params=pltpu.CompilerParams(collective_id=1, has_side_effects=True),
        name="return_parts",
    )(part)


def local(
    depth, flux_east, flux_south, river_section, bed_level, rough_class, manning_table, bank_cell
):
    owned = river_section.shape[0]
    tiles = lax.axis_size("gy")
    pos = jnp.stack([lax.axis_index("gy").astype(jnp.int32), jnp.int32(tiles)])
    below, above, nodes = exchange(
        (depth, flux_east, flux_south, bed_level, rough_class),
        river_section.reshape(1, owned),
        bank_cell,
    )
    depth, flux_east, flux_south, part = run_steps(
        manning_table,
        pos,
        depth,
        flux_east,
        flux_south,
        bed_level,
        rough_class,
        below,
        above,
        nodes,
    )
    return depth, flux_east, flux_south, return_parts(part).reshape(owned)


def solution(mesh):
    return jax.shard_map(
        local,
        mesh=mesh,
        in_specs=(
            P(("runs", "gy"), None),
            P(("runs", "gy"), None),
            P(("runs", "gy"), None),
            P(("runs", "gy")),
            P("gy", None),
            P("gy", None),
            P(),
            P(None, "gy"),
        ),
        out_specs=(
            P(("runs", "gy"), None),
            P(("runs", "gy"), None),
            P(("runs", "gy"), None),
            P(("runs", "gy")),
        ),
        check_vma=False,
    )
```

```python
import jax
import jax.numpy as jnp
from jax import lax
from jax.experimental import pallas as pl
from jax.experimental.pallas import tpu as pltpu
from jax.sharding import PartitionSpec as P

STEPS = 4
HALO = STEPS
LANES = 128

GRAV = 9.81
TSTEP = 8.0
CELL = 90.0
FLOOR = 0.05
BANK_COEF = 200.0
CELL_AREA = 8100.0
NODE_AREA = 20000.0

MESH = pl.DeviceIdType.MESH
VMEM_BYTES = 63 * 1024 * 1024
FAR = -float(1 << 24)


def send(src, dst, send_sem, recv_sem, target):
    return pltpu.make_async_remote_copy(
        src_ref=src,
        dst_ref=dst,
        send_sem=send_sem,
        recv_sem=recv_sem,
        device_id={"gy": target},
        device_id_type=MESH,
    )


def thirds(value):
    high = value.astype(jnp.bfloat16).astype(jnp.float32)
    rest = value - high
    mid = rest.astype(jnp.bfloat16).astype(jnp.float32)
    return high, mid, rest - mid


def flood_kernel(
    table,
    depth,
    flux_east,
    flux_south,
    bed_in,
    rough_in,
    section_in,
    cells_in,
    depth_out,
    east_out,
    south_out,
    section_out,
    surf,
    fe,
    fs,
    bed,
    mann,
    max_e,
    max_s,
    drag_e,
    drag_s,
    tally,
    number,
    number4,
    gained,
    partial,
    rough_own,
    up,
    down,
    below,
    above,
    mine,
    nodes,
    part,
    low,
    high,
    in_sem,
    out_sem,
    strip_ssem,
    strip_rsem,
    node_ssem,
    node_rsem,
    part_ssem,
    part_rsem,
):
    me = lax.axis_index("gy")
    tiles = lax.axis_size("gy")
    rows, columns = depth.shape
    ext = rows + 2 * HALO
    chunks = columns // LANES
    owned = nodes.shape[2]
    keep = 1.0 - TSTEP * BANK_COEF * 4.0 / NODE_AREA
    gain = TSTEP * BANK_COEF / NODE_AREA
    into = TSTEP * BANK_COEF / CELL_AREA
    offsets = (-2, -1, 1, 2)

    def there(offset):
        return (me + offset >= 0) & (me + offset < tiles)

    def absent(offset):
        return jnp.logical_not(there(offset))

    barrier = pltpu.get_barrier_semaphore()
    for offset in offsets:
        @pl.when(there(offset))
        def _():
            pl.semaphore_signal(
                barrier, inc=1, device_id={"gy": me + offset}, device_id_type=MESH
            )

    inner = slice(LANES, LANES + columns)
    loads = [
        pltpu.make_async_copy(source, target, in_sem.at[i])
        for i, (source, target) in enumerate(
            (
                (depth, surf.at[:rows, inner]),
                (flux_east, fe.at[:rows, inner]),
                (flux_south, fs.at[:rows, inner]),
                (bed_in, bed.at[:rows, inner]),
                (rough_in, rough_own),
            )
        )
    ]
    for load in loads:
        load.start()
    mine[0:1, :] = section_in[...]
    mine[1:2, :] = cells_in[0:1, :].astype(jnp.float32)

    def at(chunk, shift=0):
        start = LANES * (chunk + 1) + shift
        return slice(start, start + LANES)

    def south(value):
        return pltpu.roll(value, ext - 1, 0)

    def north(value):
        return pltpu.roll(value, 1, 0)

    for ref in (surf, fe, bed, mann, tally, number):
        ref[:, :LANES] = jnp.zeros((ext, LANES), jnp.float32)
        ref[:, LANES * (chunks + 1) :] = jnp.zeros((ext, LANES), jnp.float32)

    for load in loads:
        load.wait()
    for i, ref in enumerate((surf, fe, fs, bed)):
        up[i] = ref[:HALO, inner]
        down[i] = ref[rows - HALO : rows, inner]
    up[4] = rough_own[:HALO, :].astype(jnp.float32)
    down[4] = rough_own[rows - HALO :, :].astype(jnp.float32)

    to_prev = send(up, below, strip_ssem.at[0], strip_rsem.at[0], me - 1)
    to_next = send(down, above, strip_ssem.at[1], strip_rsem.at[1], me + 1)
    to_nodes = [
        send(mine, nodes.at[offset + 2], node_ssem.at[i], node_rsem.at[i], me - offset)
        for i, offset in enumerate(offsets)
    ]
    pl.semaphore_wait(barrier, jnp.minimum(me, 2) + jnp.minimum(tiles - 1 - me, 2))
    for i, offset in enumerate(offsets):
        @pl.when(there(-offset))
        def _():
            to_nodes[i].start()

    @pl.when(there(-1))
    def _():
        to_prev.start()

    @pl.when(there(1))
    def _():
        to_next.start()

    def roughness(rough):
        value = jnp.zeros(rough.shape, jnp.float32)
        for klass in range(table.shape[0]):
            value = jnp.where(rough == float(klass), table[klass], value)
        return value

    for c in range(chunks):
        lanes = slice(LANES * c, LANES * (c + 1))
        mann[:rows, at(c)] = roughness(rough_own[:, lanes].astype(jnp.float32))
        surf[:rows, at(c)] = surf[:rows, at(c)] + bed[:rows, at(c)]
        gained[:, at(c)] = jnp.zeros((ext, LANES), jnp.float32)

    def faces_east(span):
        for c in range(chunks):
            max_e[span, at(c)] = jnp.maximum(bed[span, at(c)], bed[span, at(c, 1)])
            mean_e = 0.5 * (mann[span, at(c)] + mann[span, at(c, 1)])
            drag_e[span, at(c)] = GRAV * TSTEP * mean_e * mean_e

    faces_east(slice(0, rows))

    nodes[2] = mine[...]
    for i, offset in enumerate(offsets):
        @pl.when(there(offset))
        def _():
            to_nodes[i].wait_recv()

        @pl.when(absent(offset))
        def _():
            nodes[offset + 2, 0:1, :] = jnp.zeros((1, owned), jnp.float32)
            nodes[offset + 2, 1:2, :] = jnp.full((1, owned), FAR, jnp.float32)

    row_id = lax.broadcasted_iota(jnp.int32, (ext, LANES), 0)
    lane_id = lax.broadcasted_iota(jnp.int32, (ext, LANES), 1)
    south_open = jnp.logical_not(
        ((row_id == ext - 1) & (me == 0)) | ((row_id == rows - 1) & (me == tiles - 1))
    )

    section = jnp.concatenate([nodes[i, 0:1, :] for i in range(5)], axis=1)
    cell = jnp.concatenate([nodes[i, 1:2, :] for i in range(5)], axis=1).astype(jnp.int32)
    local = cell - (me * rows - HALO) * columns
    valid = (local >= 0) & (local < ext * columns)
    local = jnp.where(valid, local, 0)
    from_top = ((local.astype(jnp.float32) + 0.5) * (1.0 / columns)).astype(jnp.int32)
    column = local - from_top * columns
    row = jnp.where(from_top < HALO, from_top + ext - HALO, from_top - HALO)
    place = jnp.where(valid, (column >> 7) * ext + row, -1)
    lane = column & (LANES - 1)
    total = 5 * owned
    blocks = chunks * ext
    blocks_pad = -(-blocks // LANES) * LANES
    hit = (lax.broadcasted_iota(jnp.int32, (blocks_pad, total), 0) == place)
    hit = jnp.where(hit, 1.0, 0.0).astype(jnp.bfloat16)
    lane_hit = lax.broadcasted_iota(jnp.int32, (LANES, total), 0) == lane
    parts = [jnp.where(lane_hit, part, 0.0) for part in thirds(section)]
    parts.append(jnp.where(lane_hit, 1.0, 0.0))
    weights = jnp.concatenate(parts, axis=0).astype(jnp.bfloat16)
    spread = lax.dot_general(
        hit, weights, (((1,), (1,)), ((), ())), preferred_element_type=jnp.float32
    )
    for c in range(chunks):
        block = spread[c * ext : (c + 1) * ext]
        tally[:, at(c)] = (
            block[:, :LANES] + block[:, LANES : 2 * LANES] + block[:, 2 * LANES : 3 * LANES]
        )
        number[:, at(c)] = block[:, 3 * LANES :]
    for c in range(chunks):
        number4[:, at(c)] = (
            number[:, at(c)] + number[:, at(c, -1)] + number[:, at(c, -2)] + number[:, at(c, -3)]
        )

    @pl.when(there(1))
    def _():
        to_prev.wait_recv()

    @pl.when(absent(1))
    def _():
        below[...] = jnp.zeros_like(below)

    @pl.when(there(-1))
    def _():
        to_next.wait_recv()

    @pl.when(absent(-1))
    def _():
        above[...] = jnp.zeros_like(above)

    outer = slice(rows, ext)
    for c in range(chunks):
        lanes = slice(LANES * c, LANES * (c + 1))
        halo = [
            jnp.concatenate([below[i, :, lanes], above[i, :, lanes]], axis=0) for i in range(5)
        ]
        surf[outer, at(c)] = halo[0] + halo[3]
        fe[outer, at(c)] = halo[1]
        fs[outer, at(c)] = halo[2]
        bed[outer, at(c)] = halo[3]
        mann[outer, at(c)] = roughness(halo[4])
    faces_east(outer)
    for c in range(chunks):
        bed_c, mann_c = bed[:, at(c)], mann[:, at(c)]
        max_s[:, at(c)] = jnp.maximum(bed_c, south(bed_c))
        mean_s = 0.5 * (mann_c + south(mann_c))
        drag_s[:, at(c)] = GRAV * TSTEP * mean_s * mean_s

    def face(flux, surf_a, surf_b, bed_top, drag):
        flow_depth = jnp.maximum(jnp.maximum(surf_a, surf_b) - bed_top, FLOOR)
        driven = flux - (GRAV * TSTEP / CELL) * flow_depth * (surf_b - surf_a)
        damping = 1.0 + drag * jnp.abs(flux) * jnp.exp(jnp.log(flow_depth) * (-7.0 / 3.0))
        return driven / damping

    def substep(_, carry):
        for c in reversed(range(chunks)):
            here = surf[:, at(c)]
            east = surf[:, at(c, 1)]
            new_east = face(fe[:, at(c)], here, east, max_e[:, at(c)], drag_e[:, at(c)])
            if c == chunks - 1:
                new_east = jnp.where(lane_id == LANES - 1, 0.0, new_east)
            fe[:, at(c)] = new_east
            new_south = face(
                fs[:, at(c)], here, south(here), max_s[:, at(c)], drag_s[:, at(c)]
            )
            new_south = jnp.where(south_open, new_south, 0.0)
            fs[:, at(c)] = new_south
            own = tally[:, at(c)]
            tally4 = own + tally[:, at(c, -1)] + tally[:, at(c, -2)] + tally[:, at(c, -3)]
            box = gain * (here + east + surf[:, at(c, 2)] + surf[:, at(c, 3)])
            tally[:, at(c)] = keep * own + number[:, at(c)] * box
            gained[:, at(c)] = keep * gained[:, at(c)] + box
            partial[:, at(c)] = (
                here
                + into * (tally4 - number4[:, at(c)] * here)
                + (TSTEP / CELL) * (north(new_south) - new_south - new_east)
            )
        for c in range(chunks):
            surf[:, at(c)] = partial[:, at(c)] + (TSTEP / CELL) * fe[:, at(c, -1)]
        return carry

    lax.fori_loop(0, STEPS, substep, 0)

    store_east = pltpu.make_async_copy(fe.at[:rows, inner], east_out, out_sem.at[0])
    store_south = pltpu.make_async_copy(fs.at[:rows, inner], south_out, out_sem.at[1])
    store_depth = pltpu.make_async_copy(
        partial.at[:rows, inner], depth_out, out_sem.at[2]
    )
    store_east.start()
    store_south.start()

    flat = jnp.concatenate(
        [jnp.where(row_id < rows, gained[:, at(c)], 0.0) for c in range(chunks)]
        + ([jnp.zeros((blocks_pad - blocks, LANES), jnp.float32)] if blocks_pad > blocks else []),
        axis=0,
    )
    near = slice(owned, 4 * owned)
    turned = jnp.concatenate(thirds(flat.T), axis=0).astype(jnp.bfloat16)
    picked = jnp.dot(turned, hit[:, near], preferred_element_type=jnp.float32)
    picked = picked[:LANES] + picked[LANES : 2 * LANES] + picked[2 * LANES :]
    picked = jnp.sum(jnp.where(lane_hit[:, near], picked, 0.0), axis=0, keepdims=True)
    inside = (valid & (row < rows))[:, near]
    final = jnp.where(inside, keep**STEPS * section[:, near] + picked, 0.0)
    for i in range(3):
        part[i] = final[:, i * owned : (i + 1) * owned]

    part_prev = send(part.at[0], high, part_ssem.at[0], part_rsem.at[0], me - 1)
    part_next = send(part.at[2], low, part_ssem.at[1], part_rsem.at[1], me + 1)

    @pl.when(there(-1))
    def _():
        part_prev.start()

    @pl.when(there(1))
    def _():
        part_next.start()

    for c in range(chunks):
        partial[:rows, at(c)] = surf[:rows, at(c)] - bed[:rows, at(c)]
    store_depth.start()
    section_out[...] = part[1]

    @pl.when(there(-1))
    def _():
        to_prev.wait_send()

    @pl.when(there(1))
    def _():
        to_next.wait_send()

    for i, offset in enumerate(offsets):
        @pl.when(there(-offset))
        def _():
            to_nodes[i].wait_send()

    @pl.when(there(1))
    def _():
        part_prev.wait_recv()
        section_out[...] += high[...]

    @pl.when(there(-1))
    def _():
        part_next.wait_recv()
        section_out[...] += low[...]

    @pl.when(there(-1))
    def _():
        part_prev.wait_send()

    @pl.when(there(1))
    def _():
        part_next.wait_send()

    store_east.wait()
    store_south.wait()
    store_depth.wait()


def local(
    depth, flux_east, flux_south, river_section, bed_level, rough_class, manning_table, bank_cell
):
    rows, columns = depth.shape
    owned = river_section.shape[0]
    ext = rows + 2 * HALO
    anywhere = pl.BlockSpec(memory_space=pltpu.MemorySpace.HBM)
    vmem = pl.BlockSpec(memory_space=pltpu.VMEM)
    smem = pl.BlockSpec(memory_space=pltpu.SMEM)
    tile = jax.ShapeDtypeStruct((rows, columns), jnp.float32)
    strip = pltpu.VMEM((5, HALO, columns), jnp.float32)
    line = pltpu.VMEM((1, owned), jnp.float32)
    dma = pltpu.SemaphoreType.DMA
    depth, flux_east, flux_south, section = pl.pallas_call(
        flood_kernel,
        out_shape=[tile, tile, tile, jax.ShapeDtypeStruct((1, owned), jnp.float32)],
        in_specs=[smem] + [anywhere] * 5 + [vmem] * 2,
        out_specs=[anywhere] * 3 + [vmem],
        scratch_shapes=[pltpu.VMEM((ext, columns + 2 * LANES), jnp.float32)] * 14
        + [pltpu.VMEM((rows, columns), jnp.int32)]
        + [strip] * 4
        + [
            pltpu.VMEM((2, owned), jnp.float32),
            pltpu.VMEM((5, 2, owned), jnp.float32),
            pltpu.VMEM((3, 1, owned), jnp.float32),
            line,
            line,
            dma((5,)),
            dma((3,)),
            dma((2,)),
            dma((2,)),
            dma((4,)),
            dma((4,)),
            dma((2,)),
            dma((2,)),
        ],
        compiler_params=pltpu.CompilerParams(
            collective_id=0, has_side_effects=True, vmem_limit_bytes=VMEM_BYTES
        ),
        name="flood",
    )(
        manning_table,
        depth,
        flux_east,
        flux_south,
        bed_level,
        rough_class,
        river_section.reshape(1, owned),
        bank_cell,
    )
    return depth, flux_east, flux_south, section.reshape(owned)


def solution(mesh):
    return jax.shard_map(
        local,
        mesh=mesh,
        in_specs=(
            P(("runs", "gy"), None),
            P(("runs", "gy"), None),
            P(("runs", "gy"), None),
            P(("runs", "gy")),
            P("gy", None),
            P("gy", None),
            P(),
            P(None, "gy"),
        ),
        out_specs=(
            P(("runs", "gy"), None),
            P(("runs", "gy"), None),
            P(("runs", "gy"), None),
            P(("runs", "gy")),
        ),
        check_vma=False,
    )
```

```python
import jax
import jax.numpy as jnp
from jax import lax
from jax.experimental import pallas as pl
from jax.experimental.pallas import tpu as pltpu
from jax.sharding import PartitionSpec as P

STEPS = 4
HALO = STEPS
LANES = 128

GRAV = 9.81
TSTEP = 8.0
CELL = 90.0
FLOOR = 0.05
BANK_COEF = 200.0
CELL_AREA = 8100.0
NODE_AREA = 20000.0

MESH = pl.DeviceIdType.MESH
VMEM_BYTES = 63 * 1024 * 1024
FAR = -float(1 << 24)


def send(src, dst, send_sem, recv_sem, target):
    return pltpu.make_async_remote_copy(
        src_ref=src,
        dst_ref=dst,
        send_sem=send_sem,
        recv_sem=recv_sem,
        device_id={"gy": target},
        device_id_type=MESH,
    )


def thirds(value):
    high = value.astype(jnp.bfloat16).astype(jnp.float32)
    rest = value - high
    mid = rest.astype(jnp.bfloat16).astype(jnp.float32)
    return high, mid, rest - mid


def flood_kernel(
    table,
    depth,
    flux_east,
    flux_south,
    bed_in,
    rough_in,
    section_in,
    cells_in,
    depth_out,
    east_out,
    south_out,
    section_out,
    surf,
    fe,
    fs,
    bed,
    mann,
    max_e,
    max_s,
    drag_e,
    drag_s,
    tally,
    number,
    number4,
    gained,
    partial,
    moved,
    rough_own,
    up,
    down,
    below,
    above,
    mine,
    nodes,
    part,
    low,
    high,
    in_sem,
    out_sem,
    strip_ssem,
    strip_rsem,
    node_ssem,
    node_rsem,
    part_ssem,
    part_rsem,
):
    me = lax.axis_index("gy")
    tiles = lax.axis_size("gy")
    rows, columns = depth.shape
    ext = rows + 2 * HALO
    chunks = columns // LANES
    owned = nodes.shape[2]
    keep = 1.0 - TSTEP * BANK_COEF * 4.0 / NODE_AREA
    gain = TSTEP * BANK_COEF / NODE_AREA
    into = TSTEP * BANK_COEF / CELL_AREA
    offsets = (-2, -1, 1, 2)

    def there(offset):
        return (me + offset >= 0) & (me + offset < tiles)

    def absent(offset):
        return jnp.logical_not(there(offset))

    barrier = pltpu.get_barrier_semaphore()
    for offset in offsets:
        @pl.when(there(offset))
        def _():
            pl.semaphore_signal(
                barrier, inc=1, device_id={"gy": me + offset}, device_id_type=MESH
            )

    inner = slice(LANES, LANES + columns)
    loads = [
        pltpu.make_async_copy(source, target, in_sem.at[i])
        for i, (source, target) in enumerate(
            (
                (depth, surf.at[:rows, inner]),
                (flux_east, fe.at[:rows, inner]),
                (flux_south, fs.at[:rows, inner]),
                (bed_in, bed.at[:rows, inner]),
                (rough_in, rough_own),
            )
        )
    ]
    for load in loads:
        load.start()
    mine[0:1, :] = section_in[...]
    mine[1:2, :] = cells_in[0:1, :].astype(jnp.float32)

    def at(chunk, shift=0):
        start = LANES * (chunk + 1) + shift
        return slice(start, start + LANES)

    def south(value):
        return pltpu.roll(value, ext - 1, 0)

    def north(value):
        return pltpu.roll(value, 1, 0)

    for ref in (surf, fe, bed, mann, tally, number):
        ref[:, :LANES] = jnp.zeros((ext, LANES), jnp.float32)
        ref[:, LANES * (chunks + 1) :] = jnp.zeros((ext, LANES), jnp.float32)

    for load in loads:
        load.wait()
    for i, ref in enumerate((surf, fe, fs, bed)):
        up[i] = ref[:HALO, inner]
        down[i] = ref[rows - HALO : rows, inner]
    up[4] = rough_own[:HALO, :].astype(jnp.float32)
    down[4] = rough_own[rows - HALO :, :].astype(jnp.float32)

    to_prev = send(up, below, strip_ssem.at[0], strip_rsem.at[0], me - 1)
    to_next = send(down, above, strip_ssem.at[1], strip_rsem.at[1], me + 1)
    to_nodes = [
        send(mine, nodes.at[offset + 2], node_ssem.at[i], node_rsem.at[i], me - offset)
        for i, offset in enumerate(offsets)
    ]
    pl.semaphore_wait(barrier, jnp.minimum(me, 2) + jnp.minimum(tiles - 1 - me, 2))
    for i, offset in enumerate(offsets):
        @pl.when(there(-offset))
        def _():
            to_nodes[i].start()

    @pl.when(there(-1))
    def _():
        to_prev.start()

    @pl.when(there(1))
    def _():
        to_next.start()

    def roughness(rough):
        value = jnp.zeros(rough.shape, jnp.float32)
        for klass in range(table.shape[0]):
            value = jnp.where(rough == float(klass), table[klass], value)
        return value

    for c in range(chunks):
        lanes = slice(LANES * c, LANES * (c + 1))
        mann[:rows, at(c)] = roughness(rough_own[:, lanes].astype(jnp.float32))
        surf[:rows, at(c)] = surf[:rows, at(c)] + bed[:rows, at(c)]
        gained[:, at(c)] = jnp.zeros((ext, LANES), jnp.float32)

    def faces_east(span):
        for c in range(chunks):
            max_e[span, at(c)] = jnp.maximum(bed[span, at(c)], bed[span, at(c, 1)])
            mean_e = 0.5 * (mann[span, at(c)] + mann[span, at(c, 1)])
            drag_e[span, at(c)] = GRAV * TSTEP * mean_e * mean_e

    faces_east(slice(0, rows))

    nodes[2] = mine[...]
    for i, offset in enumerate(offsets):
        @pl.when(there(offset))
        def _():
            to_nodes[i].wait_recv()

        @pl.when(absent(offset))
        def _():
            nodes[offset + 2, 0:1, :] = jnp.zeros((1, owned), jnp.float32)
            nodes[offset + 2, 1:2, :] = jnp.full((1, owned), FAR, jnp.float32)

    row_id = lax.broadcasted_iota(jnp.int32, (ext, LANES), 0)
    lane_id = lax.broadcasted_iota(jnp.int32, (ext, LANES), 1)
    south_open = jnp.logical_not(
        ((row_id == ext - 1) & (me == 0)) | ((row_id == rows - 1) & (me == tiles - 1))
    )

    def later(value, shift, carried):
        turned = pltpu.roll(value, LANES - shift, 1)
        return jnp.where(lane_id < LANES - shift, turned, carried), turned

    def earlier(value, shift, carried):
        turned = pltpu.roll(value, shift, 1)
        return jnp.where(lane_id >= shift, turned, carried), turned

    def last_four(value, carried):
        shifted, one = earlier(value, 1, carried[0])
        pair = value + shifted
        shifted, two = earlier(pair, 2, carried[1])
        return pair + shifted, (one, two)

    section = jnp.concatenate([nodes[i, 0:1, :] for i in range(5)], axis=1)
    cell = jnp.concatenate([nodes[i, 1:2, :] for i in range(5)], axis=1).astype(jnp.int32)
    local = cell - (me * rows - HALO) * columns
    valid = (local >= 0) & (local < ext * columns)
    local = jnp.where(valid, local, 0)
    from_top = ((local.astype(jnp.float32) + 0.5) * (1.0 / columns)).astype(jnp.int32)
    column = local - from_top * columns
    row = jnp.where(from_top < HALO, from_top + ext - HALO, from_top - HALO)
    place = jnp.where(valid, (column >> 7) * ext + row, -1)
    lane = column & (LANES - 1)
    total = 5 * owned
    blocks = chunks * ext
    blocks_pad = -(-blocks // LANES) * LANES
    hit = (lax.broadcasted_iota(jnp.int32, (blocks_pad, total), 0) == place)
    hit = jnp.where(hit, 1.0, 0.0).astype(jnp.bfloat16)
    lane_hit = lax.broadcasted_iota(jnp.int32, (LANES, total), 0) == lane
    parts = [jnp.where(lane_hit, part, 0.0) for part in thirds(section)]
    parts.append(jnp.where(lane_hit, 1.0, 0.0))
    weights = jnp.concatenate(parts, axis=0).astype(jnp.bfloat16)
    spread = lax.dot_general(
        hit, weights, (((1,), (1,)), ((), ())), preferred_element_type=jnp.float32
    )
    for c in range(chunks):
        block = spread[c * ext : (c + 1) * ext]
        tally[:, at(c)] = (
            block[:, :LANES] + block[:, LANES : 2 * LANES] + block[:, 2 * LANES : 3 * LANES]
        )
        number[:, at(c)] = block[:, 3 * LANES :]
    summed = (jnp.zeros((ext, LANES), jnp.float32),) * 2
    counted = summed
    for c in range(chunks):
        tally[:, at(c)], summed = last_four(tally[:, at(c)], summed)
        number4[:, at(c)], counted = last_four(number[:, at(c)], counted)

    @pl.when(there(1))
    def _():
        to_prev.wait_recv()

    @pl.when(absent(1))
    def _():
        below[...] = jnp.zeros_like(below)

    @pl.when(there(-1))
    def _():
        to_next.wait_recv()

    @pl.when(absent(-1))
    def _():
        above[...] = jnp.zeros_like(above)

    outer = slice(rows, ext)
    for c in range(chunks):
        lanes = slice(LANES * c, LANES * (c + 1))
        halo = [
            jnp.concatenate([below[i, :, lanes], above[i, :, lanes]], axis=0) for i in range(5)
        ]
        surf[outer, at(c)] = halo[0] + halo[3]
        fe[outer, at(c)] = halo[1]
        fs[outer, at(c)] = halo[2]
        bed[outer, at(c)] = halo[3]
        mann[outer, at(c)] = roughness(halo[4])
    faces_east(outer)
    for c in range(chunks):
        bed_c, mann_c = bed[:, at(c)], mann[:, at(c)]
        max_s[:, at(c)] = jnp.maximum(bed_c, south(bed_c))
        mean_s = 0.5 * (mann_c + south(mann_c))
        drag_s[:, at(c)] = GRAV * TSTEP * mean_s * mean_s

    def face(flux, surf_a, surf_b, bed_top, drag):
        flow_depth = jnp.maximum(jnp.maximum(surf_a, surf_b) - bed_top, FLOOR)
        driven = flux - (GRAV * TSTEP / CELL) * flow_depth * (surf_b - surf_a)
        damping = 1.0 + drag * jnp.abs(flux) * jnp.exp(jnp.log(flow_depth) * (-7.0 / 3.0))
        return driven / damping

    def substep(_, carry):
        blank = jnp.zeros((ext, LANES), jnp.float32)
        one, two = blank, blank
        for c in reversed(range(chunks)):
            here = surf[:, at(c)]
            east, one = later(here, 1, one)
            new_east = face(fe[:, at(c)], here, east, max_e[:, at(c)], drag_e[:, at(c)])
            if c == chunks - 1:
                new_east = jnp.where(lane_id == LANES - 1, 0.0, new_east)
            fe[:, at(c)] = new_east
            new_south = face(
                fs[:, at(c)], here, south(here), max_s[:, at(c)], drag_s[:, at(c)]
            )
            new_south = jnp.where(south_open, new_south, 0.0)
            fs[:, at(c)] = new_south
            pair = here + east
            shifted, two = later(pair, 2, two)
            box = gain * (pair + shifted)
            gained[:, at(c)] = keep * gained[:, at(c)] + box
            moved[:, at(c)] = number[:, at(c)] * box
            partial[:, at(c)] = (
                here
                + into * (tally[:, at(c)] - number4[:, at(c)] * here)
                + (TSTEP / CELL) * (north(new_south) - new_south - new_east)
            )
        west = blank
        summed = (blank, blank)
        for c in range(chunks):
            from_west, west = earlier(fe[:, at(c)], 1, west)
            surf[:, at(c)] = partial[:, at(c)] + (TSTEP / CELL) * from_west
            spill, summed = last_four(moved[:, at(c)], summed)
            tally[:, at(c)] = keep * tally[:, at(c)] + spill
        return carry

    lax.fori_loop(0, STEPS, substep, 0)

    store_east = pltpu.make_async_copy(fe.at[:rows, inner], east_out, out_sem.at[0])
    store_south = pltpu.make_async_copy(fs.at[:rows, inner], south_out, out_sem.at[1])
    store_depth = pltpu.make_async_copy(
        partial.at[:rows, inner], depth_out, out_sem.at[2]
    )
    store_east.start()
    store_south.start()

    flat = jnp.concatenate(
        [jnp.where(row_id < rows, gained[:, at(c)], 0.0) for c in range(chunks)]
        + ([jnp.zeros((blocks_pad - blocks, LANES), jnp.float32)] if blocks_pad > blocks else []),
        axis=0,
    )
    near = slice(owned, 4 * owned)
    turned = jnp.concatenate(thirds(flat.T), axis=0).astype(jnp.bfloat16)
    picked = jnp.dot(turned, hit[:, near], preferred_element_type=jnp.float32)
    picked = picked[:LANES] + picked[LANES : 2 * LANES] + picked[2 * LANES :]
    picked = jnp.sum(jnp.where(lane_hit[:, near], picked, 0.0), axis=0, keepdims=True)
    inside = (valid & (row < rows))[:, near]
    final = jnp.where(inside, keep**STEPS * section[:, near] + picked, 0.0)
    for i in range(3):
        part[i] = final[:, i * owned : (i + 1) * owned]

    part_prev = send(part.at[0], high, part_ssem.at[0], part_rsem.at[0], me - 1)
    part_next = send(part.at[2], low, part_ssem.at[1], part_rsem.at[1], me + 1)

    @pl.when(there(-1))
    def _():
        part_prev.start()

    @pl.when(there(1))
    def _():
        part_next.start()

    for c in range(chunks):
        partial[:rows, at(c)] = surf[:rows, at(c)] - bed[:rows, at(c)]
    store_depth.start()
    section_out[...] = part[1]

    @pl.when(there(-1))
    def _():
        to_prev.wait_send()

    @pl.when(there(1))
    def _():
        to_next.wait_send()

    for i, offset in enumerate(offsets):
        @pl.when(there(-offset))
        def _():
            to_nodes[i].wait_send()

    @pl.when(there(1))
    def _():
        part_prev.wait_recv()
        section_out[...] += high[...]

    @pl.when(there(-1))
    def _():
        part_next.wait_recv()
        section_out[...] += low[...]

    @pl.when(there(-1))
    def _():
        part_prev.wait_send()

    @pl.when(there(1))
    def _():
        part_next.wait_send()

    store_east.wait()
    store_south.wait()
    store_depth.wait()


def finish_kernel(a, b, c, d, a_out, b_out, c_out, d_out, held, line, in_sem, out_sem):
    sources = (a, b, c, d)
    targets = (a_out, b_out, c_out, d_out)
    stops = (held.at[0], held.at[1], held.at[2], line)
    loads = [
        pltpu.make_async_copy(sources[i], stops[i], in_sem.at[i]) for i in range(4)
    ]
    stores = [
        pltpu.make_async_copy(stops[i], targets[i], out_sem.at[i]) for i in range(4)
    ]
    for load in loads:
        load.start()
    for load, store in zip(loads, stores):
        load.wait()
        store.start()
    for store in stores:
        store.wait()


def finish(*arrays):
    anywhere = pl.BlockSpec(memory_space=pltpu.MemorySpace.HBM)
    dma = pltpu.SemaphoreType.DMA
    return pl.pallas_call(
        finish_kernel,
        out_shape=[jax.ShapeDtypeStruct(a.shape, a.dtype) for a in arrays],
        in_specs=[anywhere] * 4,
        out_specs=[anywhere] * 4,
        scratch_shapes=[
            pltpu.VMEM((3,) + arrays[0].shape, jnp.float32),
            pltpu.VMEM(arrays[3].shape, jnp.float32),
            dma((4,)),
            dma((4,)),
        ],
        compiler_params=pltpu.CompilerParams(vmem_limit_bytes=VMEM_BYTES),
        name="finish",
    )(*arrays)


def local(
    depth, flux_east, flux_south, river_section, bed_level, rough_class, manning_table, bank_cell
):
    rows, columns = depth.shape
    owned = river_section.shape[0]
    ext = rows + 2 * HALO
    anywhere = pl.BlockSpec(memory_space=pltpu.MemorySpace.HBM)
    vmem = pl.BlockSpec(memory_space=pltpu.VMEM)
    smem = pl.BlockSpec(memory_space=pltpu.SMEM)
    tile = jax.ShapeDtypeStruct((rows, columns), jnp.float32)
    strip = pltpu.VMEM((5, HALO, columns), jnp.float32)
    line = pltpu.VMEM((1, owned), jnp.float32)
    dma = pltpu.SemaphoreType.DMA
    depth, flux_east, flux_south, section = pl.pallas_call(
        flood_kernel,
        out_shape=[tile, tile, tile, jax.ShapeDtypeStruct((1, owned), jnp.float32)],
        in_specs=[smem] + [anywhere] * 5 + [vmem] * 2,
        out_specs=[anywhere] * 3 + [vmem],
        scratch_shapes=[pltpu.VMEM((ext, columns + 2 * LANES), jnp.float32)] * 15
        + [pltpu.VMEM((rows, columns), jnp.int32)]
        + [strip] * 4
        + [
            pltpu.VMEM((2, owned), jnp.float32),
            pltpu.VMEM((5, 2, owned), jnp.float32),
            pltpu.VMEM((3, 1, owned), jnp.float32),
            line,
            line,
            dma((5,)),
            dma((3,)),
            dma((2,)),
            dma((2,)),
            dma((4,)),
            dma((4,)),
            dma((2,)),
            dma((2,)),
        ],
        compiler_params=pltpu.CompilerParams(
            collective_id=0, has_side_effects=True, vmem_limit_bytes=VMEM_BYTES
        ),
        name="flood",
    )(
        manning_table,
        depth,
        flux_east,
        flux_south,
        bed_level,
        rough_class,
        river_section.reshape(1, owned),
        bank_cell,
    )
    depth, flux_east, flux_south, section = finish(depth, flux_east, flux_south, section)
    return depth, flux_east, flux_south, section.reshape(owned)


def solution(mesh):
    return jax.shard_map(
        local,
        mesh=mesh,
        in_specs=(
            P(("runs", "gy"), None),
            P(("runs", "gy"), None),
            P(("runs", "gy"), None),
            P(("runs", "gy")),
            P("gy", None),
            P("gy", None),
            P(),
            P(None, "gy"),
        ),
        out_specs=(
            P(("runs", "gy"), None),
            P(("runs", "gy"), None),
            P(("runs", "gy"), None),
            P(("runs", "gy")),
        ),
        check_vma=False,
    )
```

```python
import jax
import jax.numpy as jnp
from jax import lax
from jax.experimental import pallas as pl
from jax.experimental.pallas import tpu as pltpu
from jax.sharding import PartitionSpec as P

STEPS = 4
HALO = STEPS
LANES = 128

GRAV = 9.81
TSTEP = 8.0
CELL = 90.0
FLOOR = 0.05
BANK_COEF = 200.0
CELL_AREA = 8100.0
NODE_AREA = 20000.0

MESH = pl.DeviceIdType.MESH
VMEM_BYTES = 63 * 1024 * 1024
FAR = -float(1 << 24)


def send(src, dst, send_sem, recv_sem, target):
    return pltpu.make_async_remote_copy(
        src_ref=src,
        dst_ref=dst,
        send_sem=send_sem,
        recv_sem=recv_sem,
        device_id={"gy": target},
        device_id_type=MESH,
    )


def thirds(value):
    high = value.astype(jnp.bfloat16).astype(jnp.float32)
    rest = value - high
    mid = rest.astype(jnp.bfloat16).astype(jnp.float32)
    return high, mid, rest - mid


def flood_kernel(
    table,
    depth,
    flux_east,
    flux_south,
    bed_in,
    rough_in,
    section_in,
    cells_in,
    depth_out,
    east_out,
    south_out,
    section_out,
    surf,
    fe,
    fs,
    bed,
    mann,
    max_e,
    max_s,
    drag_e,
    drag_s,
    tally,
    number,
    number4,
    gained,
    partial,
    moved,
    rough_own,
    up,
    down,
    below,
    above,
    mine,
    nodes,
    part,
    low,
    high,
    in_sem,
    out_sem,
    strip_ssem,
    strip_rsem,
    node_ssem,
    node_rsem,
    part_ssem,
    part_rsem,
):
    me = lax.axis_index("gy")
    tiles = lax.axis_size("gy")
    rows, columns = depth.shape
    ext = rows + 2 * HALO
    chunks = columns // LANES
    owned = nodes.shape[2]
    keep = 1.0 - TSTEP * BANK_COEF * 4.0 / NODE_AREA
    gain = TSTEP * BANK_COEF / NODE_AREA
    into = TSTEP * BANK_COEF / CELL_AREA
    offsets = (-2, -1, 1, 2)

    def there(offset):
        return (me + offset >= 0) & (me + offset < tiles)

    def absent(offset):
        return jnp.logical_not(there(offset))

    barrier = pltpu.get_barrier_semaphore()
    for offset in offsets:
        @pl.when(there(offset))
        def _():
            pl.semaphore_signal(
                barrier, inc=1, device_id={"gy": me + offset}, device_id_type=MESH
            )

    inner = slice(LANES, LANES + columns)
    loads = [
        pltpu.make_async_copy(source, target, in_sem.at[i])
        for i, (source, target) in enumerate(
            (
                (depth, surf.at[:rows, inner]),
                (flux_east, fe.at[:rows, inner]),
                (flux_south, fs.at[:rows, inner]),
                (bed_in, bed.at[:rows, inner]),
                (rough_in, rough_own),
            )
        )
    ]
    for load in loads:
        load.start()
    mine[0:1, :] = section_in[...]
    mine[1:2, :] = cells_in[0:1, :].astype(jnp.float32)

    def at(chunk, shift=0):
        start = LANES * (chunk + 1) + shift
        return slice(start, start + LANES)

    def south(value):
        return pltpu.roll(value, ext - 1, 0)

    def north(value):
        return pltpu.roll(value, 1, 0)

    for ref in (surf, fe, bed, mann, tally, number):
        ref[:, :LANES] = jnp.zeros((ext, LANES), jnp.float32)
        ref[:, LANES * (chunks + 1) :] = jnp.zeros((ext, LANES), jnp.float32)

    for load in loads:
        load.wait()
    for i, ref in enumerate((surf, fe, fs, bed)):
        up[i] = ref[:HALO, inner]
        down[i] = ref[rows - HALO : rows, inner]
    up[4] = rough_own[:HALO, :].astype(jnp.float32)
    down[4] = rough_own[rows - HALO :, :].astype(jnp.float32)

    to_prev = send(up, below, strip_ssem.at[0], strip_rsem.at[0], me - 1)
    to_next = send(down, above, strip_ssem.at[1], strip_rsem.at[1], me + 1)
    to_nodes = [
        send(mine, nodes.at[offset + 2], node_ssem.at[i], node_rsem.at[i], me - offset)
        for i, offset in enumerate(offsets)
    ]
    pl.semaphore_wait(barrier, jnp.minimum(me, 2) + jnp.minimum(tiles - 1 - me, 2))
    for i, offset in enumerate(offsets):
        @pl.when(there(-offset))
        def _():
            to_nodes[i].start()

    @pl.when(there(-1))
    def _():
        to_prev.start()

    @pl.when(there(1))
    def _():
        to_next.start()

    def roughness(rough):
        value = jnp.zeros(rough.shape, jnp.float32)
        for klass in range(table.shape[0]):
            value = jnp.where(rough == float(klass), table[klass], value)
        return value

    for c in range(chunks):
        lanes = slice(LANES * c, LANES * (c + 1))
        mann[:rows, at(c)] = roughness(rough_own[:, lanes].astype(jnp.float32))
        surf[:rows, at(c)] = surf[:rows, at(c)] + bed[:rows, at(c)]
        gained[:, at(c)] = jnp.zeros((ext, LANES), jnp.float32)

    def faces_east(span):
        for c in range(chunks):
            max_e[span, at(c)] = jnp.maximum(bed[span, at(c)], bed[span, at(c, 1)])
            mean_e = 0.5 * (mann[span, at(c)] + mann[span, at(c, 1)])
            drag_e[span, at(c)] = GRAV * TSTEP * mean_e * mean_e

    faces_east(slice(0, rows))

    nodes[2] = mine[...]
    for i, offset in enumerate(offsets):
        @pl.when(there(offset))
        def _():
            to_nodes[i].wait_recv()

        @pl.when(absent(offset))
        def _():
            nodes[offset + 2, 0:1, :] = jnp.zeros((1, owned), jnp.float32)
            nodes[offset + 2, 1:2, :] = jnp.full((1, owned), FAR, jnp.float32)

    row_id = lax.broadcasted_iota(jnp.int32, (ext, LANES), 0)
    lane_id = lax.broadcasted_iota(jnp.int32, (ext, LANES), 1)
    south_open = jnp.logical_not(
        ((row_id == ext - 1) & (me == 0)) | ((row_id == rows - 1) & (me == tiles - 1))
    )

    def later(value, shift, carried):
        turned = pltpu.roll(value, LANES - shift, 1)
        return jnp.where(lane_id < LANES - shift, turned, carried), turned

    def earlier(value, shift, carried):
        turned = pltpu.roll(value, shift, 1)
        return jnp.where(lane_id >= shift, turned, carried), turned

    def last_four(value, carried):
        shifted, one = earlier(value, 1, carried[0])
        pair = value + shifted
        shifted, two = earlier(pair, 2, carried[1])
        return pair + shifted, (one, two)

    section = jnp.concatenate([nodes[i, 0:1, :] for i in range(5)], axis=1)
    cell = jnp.concatenate([nodes[i, 1:2, :] for i in range(5)], axis=1).astype(jnp.int32)
    local = cell - (me * rows - HALO) * columns
    valid = (local >= 0) & (local < ext * columns)
    local = jnp.where(valid, local, 0)
    from_top = ((local.astype(jnp.float32) + 0.5) * (1.0 / columns)).astype(jnp.int32)
    column = local - from_top * columns
    row = jnp.where(from_top < HALO, from_top + ext - HALO, from_top - HALO)
    place = jnp.where(valid, (column >> 7) * ext + row, -1)
    lane = column & (LANES - 1)
    total = 5 * owned
    blocks = chunks * ext
    blocks_pad = -(-blocks // LANES) * LANES
    hit = (lax.broadcasted_iota(jnp.int32, (blocks_pad, total), 0) == place)
    hit = jnp.where(hit, 1.0, 0.0).astype(jnp.bfloat16)
    lane_hit = lax.broadcasted_iota(jnp.int32, (LANES, total), 0) == lane
    parts = [jnp.where(lane_hit, part, 0.0) for part in thirds(section)]
    parts.append(jnp.where(lane_hit, 1.0, 0.0))
    weights = jnp.concatenate(parts, axis=0).astype(jnp.bfloat16)
    spread = lax.dot_general(
        hit, weights, (((1,), (1,)), ((), ())), preferred_element_type=jnp.float32
    )
    for c in range(chunks):
        block = spread[c * ext : (c + 1) * ext]
        tally[:, at(c)] = (
            block[:, :LANES] + block[:, LANES : 2 * LANES] + block[:, 2 * LANES : 3 * LANES]
        )
        number[:, at(c)] = block[:, 3 * LANES :]
    summed = (jnp.zeros((ext, LANES), jnp.float32),) * 2
    counted = summed
    for c in range(chunks):
        tally[:, at(c)], summed = last_four(tally[:, at(c)], summed)
        number4[:, at(c)], counted = last_four(number[:, at(c)], counted)

    @pl.when(there(1))
    def _():
        to_prev.wait_recv()

    @pl.when(absent(1))
    def _():
        below[...] = jnp.zeros_like(below)

    @pl.when(there(-1))
    def _():
        to_next.wait_recv()

    @pl.when(absent(-1))
    def _():
        above[...] = jnp.zeros_like(above)

    outer = slice(rows, ext)
    for c in range(chunks):
        lanes = slice(LANES * c, LANES * (c + 1))
        halo = [
            jnp.concatenate([below[i, :, lanes], above[i, :, lanes]], axis=0) for i in range(5)
        ]
        surf[outer, at(c)] = halo[0] + halo[3]
        fe[outer, at(c)] = halo[1]
        fs[outer, at(c)] = halo[2]
        bed[outer, at(c)] = halo[3]
        mann[outer, at(c)] = roughness(halo[4])
    faces_east(outer)
    for c in range(chunks):
        bed_c, mann_c = bed[:, at(c)], mann[:, at(c)]
        max_s[:, at(c)] = jnp.maximum(bed_c, south(bed_c))
        mean_s = 0.5 * (mann_c + south(mann_c))
        drag_s[:, at(c)] = GRAV * TSTEP * mean_s * mean_s

    def face(flux, surf_a, surf_b, bed_top, drag):
        flow_depth = jnp.maximum(jnp.maximum(surf_a, surf_b) - bed_top, FLOOR)
        driven = flux - (GRAV * TSTEP / CELL) * flow_depth * (surf_b - surf_a)
        damping = 1.0 + drag * jnp.abs(flux) * jnp.exp(jnp.log(flow_depth) * (-7.0 / 3.0))
        return driven / damping

    def substep(_, carry, nodes_too=True):
        blank = jnp.zeros((ext, LANES), jnp.float32)
        one, two = blank, blank
        for c in reversed(range(chunks)):
            here = surf[:, at(c)]
            east, one = later(here, 1, one)
            new_east = face(fe[:, at(c)], here, east, max_e[:, at(c)], drag_e[:, at(c)])
            if c == chunks - 1:
                new_east = jnp.where(lane_id == LANES - 1, 0.0, new_east)
            fe[:, at(c)] = new_east
            new_south = face(
                fs[:, at(c)], here, south(here), max_s[:, at(c)], drag_s[:, at(c)]
            )
            new_south = jnp.where(south_open, new_south, 0.0)
            fs[:, at(c)] = new_south
            if nodes_too:
                pair = here + east
                shifted, two = later(pair, 2, two)
                box = gain * (pair + shifted)
                gained[:, at(c)] = keep * gained[:, at(c)] + box
                moved[:, at(c)] = number[:, at(c)] * box
            partial[:, at(c)] = (
                here
                + into * (tally[:, at(c)] - number4[:, at(c)] * here)
                + (TSTEP / CELL) * (north(new_south) - new_south - new_east)
            )
        west = blank
        summed = (blank, blank)
        for c in range(chunks):
            from_west, west = earlier(fe[:, at(c)], 1, west)
            surf[:, at(c)] = partial[:, at(c)] + (TSTEP / CELL) * from_west
            if nodes_too:
                spill, summed = last_four(moved[:, at(c)], summed)
                tally[:, at(c)] = keep * tally[:, at(c)] + spill
        return carry

    lax.fori_loop(0, STEPS - 1, substep, 0)

    one = two = jnp.zeros((ext, LANES), jnp.float32)
    for c in reversed(range(chunks)):
        here = surf[:, at(c)]
        east, one = later(here, 1, one)
        pair = here + east
        shifted, two = later(pair, 2, two)
        gained[:, at(c)] = keep * gained[:, at(c)] + gain * (pair + shifted)

    flat = jnp.concatenate(
        [jnp.where(row_id < rows, gained[:, at(c)], 0.0) for c in range(chunks)]
        + ([jnp.zeros((blocks_pad - blocks, LANES), jnp.float32)] if blocks_pad > blocks else []),
        axis=0,
    )
    near = slice(owned, 4 * owned)
    turned = jnp.concatenate(thirds(flat.T), axis=0).astype(jnp.bfloat16)
    picked = jnp.dot(turned, hit[:, near], preferred_element_type=jnp.float32)
    picked = picked[:LANES] + picked[LANES : 2 * LANES] + picked[2 * LANES :]
    picked = jnp.sum(jnp.where(lane_hit[:, near], picked, 0.0), axis=0, keepdims=True)
    inside = (valid & (row < rows))[:, near]
    final = jnp.where(inside, keep**STEPS * section[:, near] + picked, 0.0)
    for i in range(3):
        part[i] = final[:, i * owned : (i + 1) * owned]

    part_prev = send(part.at[0], high, part_ssem.at[0], part_rsem.at[0], me - 1)
    part_next = send(part.at[2], low, part_ssem.at[1], part_rsem.at[1], me + 1)

    @pl.when(there(-1))
    def _():
        part_prev.start()

    @pl.when(there(1))
    def _():
        part_next.start()

    substep(0, 0, nodes_too=False)
    store_east = pltpu.make_async_copy(fe.at[:rows, inner], east_out, out_sem.at[0])
    store_south = pltpu.make_async_copy(fs.at[:rows, inner], south_out, out_sem.at[1])
    store_depth = pltpu.make_async_copy(
        partial.at[:rows, inner], depth_out, out_sem.at[2]
    )
    store_east.start()
    store_south.start()

    for c in range(chunks):
        partial[:rows, at(c)] = surf[:rows, at(c)] - bed[:rows, at(c)]
    store_depth.start()
    section_out[...] = part[1]

    @pl.when(there(-1))
    def _():
        to_prev.wait_send()

    @pl.when(there(1))
    def _():
        to_next.wait_send()

    for i, offset in enumerate(offsets):
        @pl.when(there(-offset))
        def _():
            to_nodes[i].wait_send()

    @pl.when(there(1))
    def _():
        part_prev.wait_recv()
        section_out[...] += high[...]

    @pl.when(there(-1))
    def _():
        part_next.wait_recv()
        section_out[...] += low[...]

    @pl.when(there(-1))
    def _():
        part_prev.wait_send()

    @pl.when(there(1))
    def _():
        part_next.wait_send()

    store_east.wait()
    store_south.wait()
    store_depth.wait()


def finish_kernel(a, b, c, d, a_out, b_out, c_out, d_out, held, line, in_sem, out_sem):
    sources = (a, b, c, d)
    targets = (a_out, b_out, c_out, d_out)
    stops = (held.at[0], held.at[1], held.at[2], line)
    loads = [
        pltpu.make_async_copy(sources[i], stops[i], in_sem.at[i]) for i in range(4)
    ]
    stores = [
        pltpu.make_async_copy(stops[i], targets[i], out_sem.at[i]) for i in range(4)
    ]
    for load in loads:
        load.start()
    for load, store in zip(loads, stores):
        load.wait()
        store.start()
    for store in stores:
        store.wait()


def finish(*arrays):
    anywhere = pl.BlockSpec(memory_space=pltpu.MemorySpace.HBM)
    dma = pltpu.SemaphoreType.DMA
    return pl.pallas_call(
        finish_kernel,
        out_shape=[jax.ShapeDtypeStruct(a.shape, a.dtype) for a in arrays],
        in_specs=[anywhere] * 4,
        out_specs=[anywhere] * 4,
        scratch_shapes=[
            pltpu.VMEM((3,) + arrays[0].shape, jnp.float32),
            pltpu.VMEM(arrays[3].shape, jnp.float32),
            dma((4,)),
            dma((4,)),
        ],
        compiler_params=pltpu.CompilerParams(vmem_limit_bytes=VMEM_BYTES),
        name="finish",
    )(*arrays)


def local(
    depth, flux_east, flux_south, river_section, bed_level, rough_class, manning_table, bank_cell
):
    rows, columns = depth.shape
    owned = river_section.shape[0]
    ext = rows + 2 * HALO
    anywhere = pl.BlockSpec(memory_space=pltpu.MemorySpace.HBM)
    vmem = pl.BlockSpec(memory_space=pltpu.VMEM)
    smem = pl.BlockSpec(memory_space=pltpu.SMEM)
    tile = jax.ShapeDtypeStruct((rows, columns), jnp.float32)
    strip = pltpu.VMEM((5, HALO, columns), jnp.float32)
    line = pltpu.VMEM((1, owned), jnp.float32)
    dma = pltpu.SemaphoreType.DMA
    depth, flux_east, flux_south, section = pl.pallas_call(
        flood_kernel,
        out_shape=[tile, tile, tile, jax.ShapeDtypeStruct((1, owned), jnp.float32)],
        in_specs=[smem] + [anywhere] * 5 + [vmem] * 2,
        out_specs=[anywhere] * 3 + [vmem],
        scratch_shapes=[pltpu.VMEM((ext, columns + 2 * LANES), jnp.float32)] * 15
        + [pltpu.VMEM((rows, columns), jnp.int32)]
        + [strip] * 4
        + [
            pltpu.VMEM((2, owned), jnp.float32),
            pltpu.VMEM((5, 2, owned), jnp.float32),
            pltpu.VMEM((3, 1, owned), jnp.float32),
            line,
            line,
            dma((5,)),
            dma((3,)),
            dma((2,)),
            dma((2,)),
            dma((4,)),
            dma((4,)),
            dma((2,)),
            dma((2,)),
        ],
        compiler_params=pltpu.CompilerParams(
            collective_id=0, has_side_effects=True, vmem_limit_bytes=VMEM_BYTES
        ),
        name="flood",
    )(
        manning_table,
        depth,
        flux_east,
        flux_south,
        bed_level,
        rough_class,
        river_section.reshape(1, owned),
        bank_cell,
    )
    depth, flux_east, flux_south, section = finish(depth, flux_east, flux_south, section)
    return depth, flux_east, flux_south, section.reshape(owned)


def solution(mesh):
    return jax.shard_map(
        local,
        mesh=mesh,
        in_specs=(
            P(("runs", "gy"), None),
            P(("runs", "gy"), None),
            P(("runs", "gy"), None),
            P(("runs", "gy")),
            P("gy", None),
            P("gy", None),
            P(),
            P(None, "gy"),
        ),
        out_specs=(
            P(("runs", "gy"), None),
            P(("runs", "gy"), None),
            P(("runs", "gy"), None),
            P(("runs", "gy")),
        ),
        check_vma=False,
    )
```
